32 devices in a mesh: dp: 2 (over y), expert: 16 (over z, x, core).
Axes of the slice: x: 2, y: 2, z: 4, core: 2. Of those that a mesh axis runs over, the one named last changes fastest.
Arguments:
- tokens: bfloat16 [1024, 2048], P('expert'), may hold values from -6 to 6
- attn_gain: float32 [2048], replicated, may hold values from 0.5 to 1.5
- w_query: bfloat16 [2048, 2048], P('expert', 'dp'), may hold values from -0.125 to 0.125
- w_key: bfloat16 [2048, 2048], P('expert', 'dp'), may hold values from -0.125 to 0.125
- w_value: bfloat16 [2048, 2048], P('expert', 'dp'), may hold values from -0.125 to 0.125
- w_out: bfloat16 [2048, 2048], P('expert', 'dp'), may hold values from -0.125 to 0.125
- cache: bfloat16 [32768, 4096], P('expert', 'dp')
- page_table: int32 [16, 16], P('expert'), may hold values from 0 to 15, each once within a row
- cache_len: int32 [16, 4], P('expert'), may hold values from 1 to 512, 1024 in all within a row
- new_len: int32 [16, 4], P('expert'), may hold values from 1 to 32, 64 in all within a row
- kv_owner: int32 [1024, 1], P('expert'), may hold values from 0 to 15; in each aligned block of 64 rows (0 to 63, 64 to 127, ...) at most 8 rows name the same one
- moe_gain: float32 [2048], replicated, may hold values from 0.5 to 1.5
- w_gate: bfloat16 [16, 2048, 1024], P('expert', None, 'dp'), may hold values from -0.125 to 0.125
- w_up: bfloat16 [16, 2048, 1024], P('expert', None, 'dp'), may hold values from -0.125 to 0.125
- w_down: bfloat16 [16, 1024, 2048], P('expert', 'dp'), may hold values from -0.1875 to 0.1875
- expert_ids: int32 [1024, 8], P('expert'), may hold values from 0 to 15, all different within a row; in each aligned block of 64 rows (0 to 63, 64 to 127, ...) at most 64 rows name the same one
- gate_weights: float32 [1024, 8], P('expert'), may hold values from 0.05 to 0.5
Outputs:
- out: bfloat16 [1024, 2048], P('expert')
- new_rows: bfloat16 [2048, 4096], P('expert', 'dp')
The draws below stay inside these ranges and needn't reach their ends.
Inputs may be any that keep to these rules, and one draw needn't show every extreme that they name: `page_table`: each row of one index of the expert axis lists every local page once; request r reserves the pages in entries r * 4 to (r+1) * 4 - 1. `cache_len`: the lengths of one index sum to 4 * 4 * 128 // 2, and one of them equals 512. `new_len`: the new tokens of one index sum to 64 and stand request by request; one request has exactly 64 // 2. `kv_owner`: among the rows of one device no owner is named more than 8 times; some owner is named exactly 8 times. `expert_ids`: each row names distinct experts; among the rows of one device no expert is named more than 64 times, a bound that some block reaches.
All inputs are finite; a program needn't handle non-finite values.
Results may differ from the reference program's by a relative error of at most 0.012.
The reference program's roundings to bfloat16 on the way (of `normed`, `probs`, `heads_out`, `moe_in`, `active` and `parts`) count: a program that leaves them out, or rounds other values in their place, can miss the bound.
Values may be sent and summed in bfloat16 or wider, within the bound.
A program may use at most 128 MiB of HBM per device.

```python
import math
import jax
import jax.numpy as jnp
import numpy as np
from jax import lax

D = 2048
HEADS = 16
HD = 128
FF = 1024
TOP = 8
TOK_DEV = 64
REQ_DEV = 4
PAGE = 128
PAGES_REQ = 4
PAGES_DEV = 16
EXPERTS = 16
TOKENS = 1024
CAP = 64
KCAP = 8
POOL_DEV = 128
N_DP = 2
N_EXPERT = 16


def draw_cache(key, part):
    row_total = N_EXPERT * PAGES_DEV * PAGE
    feat_total = 2 * HEADS * HD
    base = jax.random.normal(key, (row_total, feat_total), jnp.float32)
    return base.astype(jnp.bfloat16)


def block_levels(rng, dims, shards, smallest, high):
    level = 1.0
    for dim, blocks in shards:
        heights = jax.random.uniform(jax.random.fold_in(jax.random.fold_in(rng, 6), dim), (blocks,), jnp.float32, smallest / len(shards), high / len(shards))
        level = level * jnp.repeat(jnp.exp(heights), dims[dim] // blocks).reshape((-1,) + (1,) * (len(dims) - 1 - dim))
    return level


def profile(number_of, total, most, slope):
    weights = [(1 << 20) // math.isqrt(standing ** slope) + 1 for standing in range(2, number_of + 1)]
    surplus, given = total - most - (number_of - 1), [1] * (number_of - 1)
    while surplus > 0:
        free = [i for i in range(number_of - 1) if given[i] < most]
        whole, left = sum([weights[i] for i in free]), surplus
        for i in free:
            more = min(most - given[i], max(1, left * weights[i] // whole), surplus)
            given[i] = given[i] + more
            surplus = surplus - more
    return np.array([most] + given)


def ragged_sizes(key, amount, total, bound, lean):
    if amount == 2:
        one = jax.random.randint(key, (), max(1, total - bound), min(bound, total - 1) + 1)
        return jnp.stack([one, total - one])
    tallies = jnp.asarray(profile(amount, total, bound, lean), jnp.int32)
    couples = (amount - 1) // 2
    source_of, receiver = tallies[1:1 + 2 * couples:2], tallies[2:2 + 2 * couples:2]
    margin = jnp.minimum(source_of - 1, bound - receiver)
    shifted = jax.random.randint(jax.random.fold_in(key, 1), (couples,), 0, 1 << 20) % (margin + 1)
    tallies = tallies.at[1:1 + 2 * couples:2].set(source_of - shifted).at[2:2 + 2 * couples:2].set(receiver + shifted)
    return tallies[jax.random.permutation(jax.random.fold_in(key, 2), amount)]


def assign_block(key, own, number, rows, count, top, reach, lean):
    sequence = jax.random.permutation(key, count)
    crowded, ordinary = load_shares(count, rows * top, reach, lean, True), load_shares(count, rows * top, reach, lean, False)
    places = jnp.arange(count)

    def named(sizes, offset_by):
        used = int((sizes > 0).sum())
        fixed = max(1, used // 4)
        shifted = fixed + (places - fixed + offset_by * (used - fixed)) % max(1, count - fixed)
        return jnp.zeros((count,), jnp.int32).at[sequence[jnp.where(places < fixed, places, shifted)]].set(jnp.asarray(sizes, jnp.int32))

    sizes = jnp.where(number % 4 == 0, named(crowded, number // 4), named(ordinary, number - number // 4 - 1))
    mixed = jax.random.permutation(jax.random.fold_in(own, 3), count)
    giver, taker = mixed[0:count // 2 * 2:2], mixed[1:count // 2 * 2:2]
    room = jnp.minimum(sizes[giver] - 1, reach - sizes[taker]) // 2
    room = jnp.where((giver == sequence[0]) | (taker == sequence[0]) | (sizes[taker] == 0), 0, jnp.maximum(room, 0))
    shifted = jax.random.randint(jax.random.fold_in(own, 4), (count // 2,), 0, 1 << 20) % (room + 1)
    sizes = sizes.at[giver].add(-shifted).at[taker].add(shifted)
    items = jnp.searchsorted(jnp.cumsum(sizes), jnp.arange(rows * top), side="right").astype(jnp.int32)
    grid = items.reshape(top, rows).T
    grid = grid[jax.random.permutation(jax.random.fold_in(own, 1), rows)]
    offset_by = jax.random.randint(jax.random.fold_in(own, 2), (rows, 1), 0, top)
    return jnp.take_along_axis(grid, (jnp.arange(top)[None, :] + offset_by) % top, axis=1)


def load_shares(amount, total, reach, skew, full):
    portions = [(1 << 20) // math.isqrt(standing ** skew) + 1 for standing in range(1, amount + 1)]
    largest = reach if full else min(reach, max(-(-total // amount), total * portions[0] // sum(portions)))
    least = 1 if total - largest >= amount - 1 else 0
    given, rest = [largest] + [least] * (amount - 1), total - largest - least * (amount - 1)
    while rest > 0:
        candidates = [i for i in range(1, amount) if given[i] < largest] or [i for i in range(1, amount) if given[i] < reach]
        mass, left = sum([portions[i] for i in candidates]), rest
        for i in candidates:
            addition = min(reach - given[i], max(1, left * portions[i] // mass), rest)
            given[i] = given[i] + addition
            rest = rest - addition
    return np.array(given)


def scatter_about(stream_key, dims, width, most, cuts=(), kind=jnp.bfloat16):
    level = block_levels(stream_key, dims, cuts, -0.22, 0.18) if cuts else 1.0
    entries = jax.random.normal(stream_key, dims, jnp.float32) * width * level
    return jnp.minimum(jnp.maximum(entries, -most), most).astype(kind)


def setup_inputs(seed: int = 0) -> dict:
    key_of = jax.random.split(jax.random.key(seed), 18)
    tokens = scatter_about(key_of[0], (TOKENS, D), 1.0, 6.0, ((0, 16),))
    attn_gain = jnp.clip(1.0 + 0.1 * jax.random.normal(key_of[1], (D,), jnp.float32), 0.5, 1.5)
    w_query = scatter_about(key_of[2], (D, HEADS * HD), D ** -0.5, 0.125, ((0, 16), (1, 2)))
    w_key = scatter_about(key_of[3], (D, HEADS * HD), D ** -0.5, 0.125, ((0, 16), (1, 2)))
    w_value = scatter_about(key_of[4], (D, HEADS * HD), D ** -0.5, 0.125, ((0, 16), (1, 2)))
    w_out = scatter_about(key_of[5], (D, HEADS * HD), (HEADS * HD) ** -0.5, 0.125, ((0, 16), (1, 2)))
    cache = draw_cache(jax.random.fold_in(key_of[17], 71), 0)
    page_table = jax.vmap(lambda own: jax.random.permutation(own, PAGES_DEV))(jax.random.split(key_of[7], N_EXPERT)).reshape((N_EXPERT, PAGES_DEV)).astype(jnp.int32)
    cache_len = jax.vmap(lambda own: ragged_sizes(own, REQ_DEV, REQ_DEV * PAGES_REQ * PAGE // 2, PAGES_REQ * PAGE, 2))(jax.random.split(key_of[8], N_EXPERT)).reshape((N_EXPERT, REQ_DEV)).astype(jnp.int32)
    new_len = jax.vmap(lambda own: ragged_sizes(own, REQ_DEV, TOK_DEV, TOK_DEV // 2, 2))(jax.random.split(key_of[9], N_EXPERT)).reshape((N_EXPERT, REQ_DEV)).astype(jnp.int32)
    kv_owner_keys = jax.random.split(jax.random.fold_in(key_of[10], 1), TOKENS // TOK_DEV)
    kv_owner_turns = jax.random.permutation(jax.random.fold_in(key_of[10], 3), TOKENS // TOK_DEV)
    kv_owner = jax.vmap(lambda own, number: assign_block(jax.random.fold_in(key_of[10], 2), own, number, TOK_DEV, N_EXPERT, 1, KCAP, 1))(kv_owner_keys, kv_owner_turns).reshape((TOKENS, 1))
    moe_gain = jnp.clip(1.0 + 0.1 * jax.random.normal(key_of[11], (D,), jnp.float32), 0.5, 1.5)
    w_gate = scatter_about(key_of[12], (EXPERTS, D, FF), D ** -0.5, 0.125, ((0, 16), (2, 2)))
    w_up = scatter_about(key_of[13], (EXPERTS, D, FF), D ** -0.5, 0.125, ((0, 16), (2, 2)))
    w_down = scatter_about(key_of[14], (EXPERTS, FF, D), FF ** -0.5, 0.1875, ((0, 16), (1, 2)))
    expert_ids_keys = jax.random.split(jax.random.fold_in(key_of[15], 1), TOKENS // TOK_DEV)
    expert_ids_turns = jax.random.permutation(jax.random.fold_in(key_of[15], 3), TOKENS // TOK_DEV)
    expert_ids = jax.vmap(lambda own, number: assign_block(jax.random.fold_in(key_of[15], 2), own, number, TOK_DEV, EXPERTS, TOP, CAP, 2))(expert_ids_keys, expert_ids_turns).reshape((TOKENS, TOP))
    gate_weights = jnp.clip(jnp.exp(math.log(0.5) - 2.3025851 * jax.random.uniform(key_of[16], (TOKENS, TOP), jnp.float32) ** block_levels(key_of[16], (TOKENS, TOP), ((0, 16),), -0.2, 0.2)), 0.05, 0.5)
    return {"tokens": tokens, "attn_gain": attn_gain, "w_query": w_query, "w_key": w_key, "w_value": w_value, "w_out": w_out, "cache": cache, "page_table": page_table, "cache_len": cache_len, "new_len": new_len, "kv_owner": kv_owner, "moe_gain": moe_gain, "w_gate": w_gate, "w_up": w_up, "w_down": w_down, "expert_ids": expert_ids, "gate_weights": gate_weights}


EPSILON = 1e-05

def norm_rows(row_data, gain_vec):
    mean_sq = lax.optimization_barrier(jnp.mean(row_data * row_data, axis=-1, keepdims=True))
    return (row_data * lax.rsqrt(mean_sq + EPSILON) * gain_vec).astype(jnp.bfloat16)

def route_rank(route_ids, block_rows, id_range):
    row_total = route_ids.shape[0]
    labels = jnp.arange(id_range, dtype=jnp.int32)
    counts = lax.optimization_barrier(jnp.sum((route_ids[:, :, None] == labels[None, None, :]).astype(jnp.int32), axis=1)).astype(jnp.int32)
    counts = counts.reshape(row_total // block_rows, block_rows, id_range)
    before = (jnp.cumsum(counts, axis=1).astype(jnp.int32) - counts).reshape(row_total, id_range)
    return jnp.take_along_axis(before, route_ids, axis=1).astype(jnp.int32)

def key_masks(table_row, cache_lens, new_lens, row_count, page_size):
    req_count = cache_lens.shape[0]
    pages_here = table_row.shape[0]
    per_request = pages_here // req_count
    slot_ids = jnp.arange(pages_here, dtype=jnp.int32)
    matches = (table_row[:, None] == slot_ids[None, :]).astype(jnp.int32)
    slot_of_page = lax.optimization_barrier(jnp.sum(matches * slot_ids[:, None], axis=0)).astype(jnp.int32)
    page_request = slot_of_page // per_request
    page_start = slot_of_page % per_request * page_size
    key_request = jnp.repeat(page_request, page_size)
    key_position = jnp.repeat(page_start, page_size) + jnp.tile(jnp.arange(page_size, dtype=jnp.int32), pages_here)
    request_ids = jnp.arange(req_count, dtype=jnp.int32)
    key_length = lax.optimization_barrier(jnp.sum((key_request[:, None] == request_ids[None, :]).astype(jnp.int32) * cache_lens[None, :], axis=1)).astype(jnp.int32)
    request_ends = jnp.cumsum(new_lens).astype(jnp.int32)
    tok_ids = jnp.arange(row_count, dtype=jnp.int32)
    tok_request = lax.optimization_barrier(jnp.sum((tok_ids[:, None] >= request_ends[None, :]).astype(jnp.int32), axis=1)).astype(jnp.int32)
    cached = (tok_request[:, None] == key_request[None, :]) & (key_position < key_length)[None, :]
    fresh_mask = tok_request[:, None] == tok_request[None, :]
    return jnp.concatenate([cached, fresh_mask], axis=1)

def attention_block(token_rows, cache_rows, table_row, cache_lens, new_lens, attn_gain, w_query, w_key, w_value, w_out, moe_gain):
    row_count = token_rows.shape[0]
    cache_count = cache_rows.shape[0]
    per_group = HEADS // N_DP
    resid_in = token_rows.astype(jnp.float32)
    normed = norm_rows(resid_in, attn_gain)
    queries = jnp.dot(normed, w_query, preferred_element_type=jnp.float32).astype(jnp.bfloat16)
    new_keys = jnp.dot(normed, w_key, preferred_element_type=jnp.float32).astype(jnp.bfloat16)
    new_values = jnp.dot(normed, w_value, preferred_element_type=jnp.float32).astype(jnp.bfloat16)
    split_cache = cache_rows.reshape(cache_count, N_DP, 2, per_group, HD)
    all_keys = jnp.concatenate([split_cache[:, :, 0].reshape(cache_count, HEADS, HD), new_keys.reshape(row_count, HEADS, HD)], axis=0).astype(jnp.float32)
    all_values = jnp.concatenate([split_cache[:, :, 1].reshape(cache_count, HEADS, HD), new_values.reshape(row_count, HEADS, HD)], axis=0).astype(jnp.float32)
    scores = jnp.einsum('thc,rhc->htr', queries.reshape(row_count, HEADS, HD).astype(jnp.float32), all_keys) * HD ** (-0.5)
    valid_mask = key_masks(table_row, cache_lens, new_lens, row_count, PAGE)
    scores = jnp.where(valid_mask[None, :, :], scores, -1e+30)
    highest = lax.optimization_barrier(jnp.max(scores, axis=-1, keepdims=True))
    weights = jnp.exp(scores - highest)
    probs = (weights / lax.optimization_barrier(jnp.sum(weights, axis=-1, keepdims=True))).astype(jnp.bfloat16)
    heads_out = jnp.einsum('htr,rhc->thc', probs.astype(jnp.float32), all_values).astype(jnp.bfloat16).reshape(row_count, HEADS * HD)
    attn_out = jnp.dot(heads_out, w_out.T, preferred_element_type=jnp.float32)
    residual = resid_in + attn_out
    moe_in = norm_rows(residual, moe_gain)
    kv_rows = jnp.stack([new_keys.reshape(row_count, N_DP, per_group * HD), new_values.reshape(row_count, N_DP, per_group * HD)], axis=2).reshape(row_count, 2 * HEADS * HD)
    return (residual, moe_in, kv_rows)

def reference(tokens, attn_gain, w_query, w_key, w_value, w_out, cache, page_table, cache_len, new_len, kv_owner, moe_gain, w_gate, w_up, w_down, expert_ids, gate_weights):

    def per_device(pieces):
        return attention_block(pieces[0], pieces[1], pieces[2], pieces[3], pieces[4], attn_gain, w_query, w_key, w_value, w_out, moe_gain)
    residual, moe_in, kv_rows = lax.map(per_device, (tokens.reshape(N_EXPERT, TOK_DEV, D), cache.reshape(N_EXPERT, -1, cache.shape[1]), page_table, cache_len, new_len))
    residual = residual.reshape(N_EXPERT * TOK_DEV, D)
    moe_flat = moe_in.reshape(N_EXPERT * TOK_DEV, D)
    kv_flat = kv_rows.reshape(N_EXPERT * TOK_DEV, kv_rows.shape[-1])
    token_ids = jnp.arange(N_EXPERT * TOK_DEV, dtype=jnp.int32)
    sources = token_ids // TOK_DEV
    kv_rank = route_rank(kv_owner, TOK_DEV, N_EXPERT)[:, 0]
    dest_rows = kv_owner[:, 0] * POOL_DEV + sources * KCAP + kv_rank
    new_rows = jnp.zeros((N_EXPERT * POOL_DEV, kv_flat.shape[1]), jnp.bfloat16).at[dest_rows].set(kv_flat)
    slot_rank = route_rank(expert_ids, TOK_DEV, EXPERTS)
    columns = sources[:, None] * CAP + slot_rank
    holders = jnp.broadcast_to(token_ids[:, None], expert_ids.shape)
    index_table = jnp.zeros((EXPERTS, N_EXPERT * CAP), jnp.int32).at[expert_ids, columns].set(holders)
    gate_table = jnp.zeros((EXPERTS, N_EXPERT * CAP), jnp.float32).at[expert_ids, columns].set(gate_weights)
    slice_width = FF // N_DP

    def one_expert(running, pieces):
        row_index, gate_col, gate_mat, up_mat, down_mat = pieces
        picked = moe_flat[row_index]
        gate_proj = jnp.dot(picked, gate_mat, preferred_element_type=jnp.float32)
        up_proj = jnp.dot(picked, up_mat, preferred_element_type=jnp.float32)
        active = (jax.nn.silu(gate_proj) * up_proj).astype(jnp.bfloat16)
        parts = jnp.einsum('rnf,nfd->nrd', active.reshape(-1, N_DP, slice_width).astype(jnp.float32), down_mat.reshape(N_DP, slice_width, D).astype(jnp.float32)).astype(jnp.bfloat16)
        contrib = lax.optimization_barrier(jnp.sum(parts.astype(jnp.float32), axis=0))
        return (running.at[row_index].add(gate_col[:, None] * contrib), None)
    moe_total, unused = lax.scan(one_expert, jnp.zeros((N_EXPERT * TOK_DEV, D), jnp.float32), (index_table, gate_table, w_gate, w_up, w_down))
    out = (residual + moe_total).astype(jnp.bfloat16)
    return (out, new_rows)
```

```python
import jax
import jax.numpy as jnp
from jax import lax
from jax.sharding import PartitionSpec as P

HD = 128
PAGE = 128


EPSILON = 1e-05


def norm_rows(row_data, gain_vec):
    mean_sq = jnp.mean(row_data * row_data, axis=-1, keepdims=True)
    return (row_data * lax.rsqrt(mean_sq + EPSILON) * gain_vec).astype(jnp.bfloat16)


def owner_rank(owners):
    ids = jnp.arange(owners.shape[0], dtype=jnp.int32)
    same = (owners[:, None] == owners[None, :]) & (ids[None, :] < ids[:, None])
    return jnp.sum(same.astype(jnp.int32), axis=1)


def key_masks(table_row, cache_lens, new_lens, row_count, page_size):
    req_count = cache_lens.shape[0]
    pages_here = table_row.shape[0]
    per_request = pages_here // req_count
    slot_ids = jnp.arange(pages_here, dtype=jnp.int32)
    matches = (table_row[:, None] == slot_ids[None, :]).astype(jnp.int32)
    slot_of_page = jnp.sum(matches * slot_ids[:, None], axis=0)
    page_request = slot_of_page // per_request
    page_start = slot_of_page % per_request * page_size
    key_request = jnp.repeat(page_request, page_size)
    key_position = jnp.repeat(page_start, page_size) + jnp.tile(
        jnp.arange(page_size, dtype=jnp.int32), pages_here
    )
    request_ids = jnp.arange(req_count, dtype=jnp.int32)
    key_length = jnp.sum(
        (key_request[:, None] == request_ids[None, :]).astype(jnp.int32) * cache_lens[None, :],
        axis=1,
    )
    request_ends = jnp.sum(
        jnp.where(request_ids[None, :] <= request_ids[:, None], new_lens[None, :], 0), axis=1
    )
    tok_ids = jnp.arange(row_count, dtype=jnp.int32)
    tok_request = jnp.sum((tok_ids[:, None] >= request_ends[None, :]).astype(jnp.int32), axis=1)
    cached = (tok_request[:, None] == key_request[None, :]) & (key_position < key_length)[None, :]
    fresh_mask = tok_request[:, None] == tok_request[None, :]
    return jnp.concatenate([cached, fresh_mask], axis=1)


def local(
    tokens,
    attn_gain,
    w_query,
    w_key,
    w_value,
    w_out,
    cache,
    page_table,
    cache_len,
    new_len,
    kv_owner,
    moe_gain,
    w_gate,
    w_up,
    w_down,
    expert_ids,
    gate_weights,
):
    row_count, model_width = tokens.shape
    n_expert = lax.axis_size("expert")
    local_experts = w_gate.shape[0]
    experts_all = n_expert * local_experts
    kv_cap = max(2, 2 * row_count // n_expert)
    head_group = w_query.shape[1] // HD
    full_query, full_key, full_value, full_out = (
        lax.all_gather(w_query, "expert", axis=0, tiled=True),
        lax.all_gather(w_key, "expert", axis=0, tiled=True),
        lax.all_gather(w_value, "expert", axis=0, tiled=True),
        lax.all_gather(w_out, "expert", axis=0, tiled=True),
    )
    resid_in = tokens.astype(jnp.float32)
    normed = norm_rows(resid_in, attn_gain)
    queries = jnp.dot(normed, full_query, preferred_element_type=jnp.float32).astype(jnp.bfloat16)
    new_keys = jnp.dot(normed, full_key, preferred_element_type=jnp.float32).astype(jnp.bfloat16)
    new_values = jnp.dot(normed, full_value, preferred_element_type=jnp.float32).astype(
        jnp.bfloat16
    )
    cache_count = cache.shape[0]
    split_cache = cache.reshape(cache_count, 2, head_group, HD)
    all_keys = jnp.concatenate(
        [split_cache[:, 0], new_keys.reshape(row_count, head_group, HD)], axis=0
    )
    all_values = jnp.concatenate(
        [split_cache[:, 1], new_values.reshape(row_count, head_group, HD)], axis=0
    )
    scores = jnp.einsum(
        "thc,rhc->htr",
        queries.reshape(row_count, head_group, HD),
        all_keys,
        preferred_element_type=jnp.float32,
    ) * HD ** (-0.5)
    valid_mask = key_masks(page_table[0], cache_len[0], new_len[0], row_count, PAGE)
    scores = jnp.where(valid_mask[None, :, :], scores, -1e30)
    highest = jnp.max(scores, axis=-1, keepdims=True)
    weights = jnp.exp(scores - highest)
    probs = (weights / jnp.sum(weights, axis=-1, keepdims=True)).astype(jnp.bfloat16)
    heads_out = (
        jnp.einsum("htr,rhc->thc", probs, all_values, preferred_element_type=jnp.float32)
        .astype(jnp.bfloat16)
        .reshape(row_count, head_group * HD)
    )
    attn_part = jnp.einsum("tc,dc->td", heads_out, full_out, preferred_element_type=jnp.float32)
    attn_out = lax.psum(attn_part.astype(jnp.bfloat16), "dp").astype(jnp.float32)
    residual = resid_in + attn_out
    moe_in = norm_rows(residual, moe_gain)
    kv_row = jnp.concatenate([new_keys, new_values], axis=1)
    kv_slot = kv_owner[:, 0] * kv_cap + owner_rank(kv_owner[:, 0])
    slots = jnp.arange(n_expert * kv_cap, dtype=jnp.int32)
    kv_buffer = jnp.dot(
        (slots[:, None] == kv_slot[None, :]).astype(jnp.bfloat16),
        kv_row,
        preferred_element_type=jnp.float32,
    ).astype(jnp.bfloat16)
    labels = jnp.arange(experts_all, dtype=jnp.int32)
    gates = jnp.sum(
        jnp.where(expert_ids[:, :, None] == labels, gate_weights[:, :, None], 0.0), axis=1
    )
    new_rows = lax.all_to_all(
        kv_buffer.reshape(n_expert, kv_cap, -1), "expert", split_axis=0, concat_axis=0, tiled=True
    ).reshape(n_expert * kv_cap, -1)
    all_gates = lax.all_gather(gates, "expert", axis=0, tiled=True)
    rows = lax.all_gather(moe_in, "expert", axis=0, tiled=True)
    first = lax.axis_index("expert") * local_experts
    gated = 0.0
    for local_id in range(local_experts):
        gate_proj = jnp.dot(rows, w_gate[local_id], preferred_element_type=jnp.float32)
        up_proj = jnp.dot(rows, w_up[local_id], preferred_element_type=jnp.float32)
        active = (jax.nn.silu(gate_proj) * up_proj).astype(jnp.bfloat16)
        part = jnp.dot(active, w_down[local_id], preferred_element_type=jnp.float32)
        part = part.astype(jnp.bfloat16).astype(jnp.float32)
        mine = jnp.sum(jnp.where(labels == first + local_id, all_gates, 0.0), axis=1)
        gated = gated + part * mine[:, None]
    moe_part = lax.psum_scatter(
        gated.astype(jnp.bfloat16), "expert", scatter_dimension=0, tiled=True
    )
    moe_total = lax.psum(moe_part, "dp").astype(jnp.float32)
    out = (residual + moe_total).astype(jnp.bfloat16)
    return (out, new_rows)


def solution(mesh):
    placed = (
        P("expert", None),
        P(),
        P("expert", "dp"),
        P("expert", "dp"),
        P("expert", "dp"),
        P("expert", "dp"),
        P("expert", "dp"),
        P("expert", None),
        P("expert", None),
        P("expert", None),
        P("expert", None),
        P(),
        P("expert", None, "dp"),
        P("expert", None, "dp"),
        P("expert", "dp", None),
        P("expert", None),
        P("expert", None),
    )
    return jax.shard_map(
        local,
        mesh=mesh,
        in_specs=placed,
        out_specs=(P("expert", None), P("expert", "dp")),
        check_vma=False,
    )
```

```python
import functools

import jax
import jax.numpy as jnp
from jax import lax
from jax.experimental import pallas as pl
from jax.experimental.pallas import tpu as pltpu
from jax.sharding import PartitionSpec as P

HD = 128
PAGE = 128
VMEM_LIMIT = 56 * 1024 * 1024


EPSILON = 1e-05


def norm_rows(row_data, gain_vec):
    mean_sq = jnp.mean(row_data * row_data, axis=-1, keepdims=True)
    return (row_data * lax.rsqrt(mean_sq + EPSILON) * gain_vec).astype(jnp.bfloat16)


def owner_rank(owners):
    ids = jnp.arange(owners.shape[0], dtype=jnp.int32)
    same = (owners[:, None] == owners[None, :]) & (ids[None, :] < ids[:, None])
    return jnp.sum(same.astype(jnp.int32), axis=1)


def key_masks(table_row, cache_lens, new_lens, row_count, page_size):
    req_count = cache_lens.shape[0]
    pages_here = table_row.shape[0]
    per_request = pages_here // req_count
    slot_ids = jnp.arange(pages_here, dtype=jnp.int32)
    matches = (table_row[:, None] == slot_ids[None, :]).astype(jnp.int32)
    slot_of_page = jnp.sum(matches * slot_ids[:, None], axis=0)
    page_request = slot_of_page // per_request
    page_start = slot_of_page % per_request * page_size
    key_request = jnp.repeat(page_request, page_size)
    key_position = jnp.repeat(page_start, page_size) + jnp.tile(
        jnp.arange(page_size, dtype=jnp.int32), pages_here
    )
    request_ids = jnp.arange(req_count, dtype=jnp.int32)
    key_length = jnp.sum(
        (key_request[:, None] == request_ids[None, :]).astype(jnp.int32) * cache_lens[None, :],
        axis=1,
    )
    request_ends = jnp.sum(
        jnp.where(request_ids[None, :] <= request_ids[:, None], new_lens[None, :], 0), axis=1
    )
    tok_ids = jnp.arange(row_count, dtype=jnp.int32)
    tok_request = jnp.sum((tok_ids[:, None] >= request_ends[None, :]).astype(jnp.int32), axis=1)
    cached = (tok_request[:, None] == key_request[None, :]) & (key_position < key_length)[None, :]
    fresh_mask = tok_request[:, None] == tok_request[None, :]
    return jnp.concatenate([cached, fresh_mask], axis=1)


def grid_place(nx):
    me = lax.axis_index("expert")
    return me // (2 * nx), (me // 2) % nx, me % 2


def remote(src, dst, send_sem, recv_sem, device):
    return pltpu.make_async_remote_copy(
        src_ref=src,
        dst_ref=dst,
        send_sem=send_sem,
        recv_sem=recv_sem,
        device_id=device,
        device_id_type=pl.DeviceIdType.MESH,
    )


def greet(nz, nx, ndp, z, x, c):
    def index(z_to, x_to, c_to):
        return (lax.axis_index("dp"), (z_to * nx + x_to) * 2 + c_to)

    barrier = pltpu.get_barrier_semaphore()
    peers = [index(z, x, 1 - c)]
    peers += [index(z, (x + k) % nx, c) for k in range(1, nx)]
    peers += [index((z + k) % nz, x, c) for k in range(1, nz)]
    peers += [
        ((lax.axis_index("dp") + k) % ndp, lax.axis_index("expert")) for k in range(1, ndp)
    ]
    for peer in peers:
        pl.semaphore_signal(barrier, inc=1, device_id=peer, device_id_type=pl.DeviceIdType.MESH)
    pl.semaphore_wait(barrier, len(peers))
    return index


def dp_sum(ndp, ybuf, ysend, yrecv):
    mine = lax.axis_index("dp")
    expert = lax.axis_index("expert")
    copies = []
    for k in range(1, ndp):
        copy = remote(
            ybuf.at[mine],
            ybuf.at[mine],
            ysend.at[k - 1],
            yrecv.at[k - 1],
            ((mine + k) % ndp, expert),
        )
        copy.start()
        copies.append(copy)
    for copy in copies:
        copy.wait()
    total = ybuf[0].astype(jnp.float32)
    for d in range(1, ndp):
        total = total + ybuf[d].astype(jnp.float32)
    return total


def scatter_kernel(
    nz, nx, ndp, part, out, cbuf, xbuf, zbuf, ybuf,
    csend, crecv, xsend, xrecv, zsend, zrecv, ysend, yrecv,
):
    z, x, c = grid_place(nx)
    index = greet(nz, nx, ndp, z, x, c)

    def to_core(j, k):
        zz, xx = (z + j) % nz, (x + k) % nx
        return remote(
            part.at[zz, xx, 1 - c], cbuf.at[zz, xx], csend.at[j, k], crecv.at[j, k],
            index(z, x, 1 - c),
        )

    def to_x(j, k):
        zz, xx = (z + j) % nz, (x + k) % nx
        return remote(
            cbuf.at[zz, xx], xbuf.at[k - 1, zz], xsend.at[k - 1, j], xrecv.at[k - 1, j],
            index(z, xx, c),
        )

    def to_z(j):
        zz = (z + j) % nz
        return remote(
            cbuf.at[zz, x], zbuf.at[j - 1], zsend.at[j - 1], zrecv.at[j - 1], index(zz, x, c)
        )

    def order(i):
        return (i + 1) % nz

    def start_core(i, carry):
        for k in range(1, nx):
            to_core(order(i), k).start()
        return carry

    def start_own(i, carry):
        to_core(order(i), 0).start()
        return carry

    def x_step(i, carry):
        j = order(i)
        zz = (z + j) % nz
        for k in range(1, nx):
            xx = (x + k) % nx
            to_core(j, k).wait_recv()
            summed = cbuf[zz, xx].astype(jnp.float32) + part[zz, xx, c].astype(jnp.float32)
            cbuf[zz, xx] = summed.astype(jnp.bfloat16)
            to_x(j, k).start()
        return carry

    def column(j):
        zz = (z + j) % nz
        to_core(j, 0).wait_recv()
        summed = cbuf[zz, x].astype(jnp.float32) + part[zz, x, c].astype(jnp.float32)
        for k in range(1, nx):
            to_x(j, k).wait_recv()
            summed = summed + xbuf[k - 1, zz].astype(jnp.float32)
        return zz, summed

    def z_step(j, carry):
        zz, summed = column(j)
        cbuf[zz, x] = summed.astype(jnp.bfloat16)
        to_z(j).start()
        return carry

    lax.fori_loop(0, nz, start_core, 0)
    lax.fori_loop(0, nz, start_own, 0)
    lax.fori_loop(0, nz, x_step, 0)
    lax.fori_loop(1, nz, z_step, 0)
    _, total = column(0)
    for j in range(1, nz):
        to_z(j).wait_recv()
        total = total + zbuf[j - 1].astype(jnp.float32)
    if ndp > 1:
        ybuf[lax.axis_index("dp")] = total.astype(jnp.bfloat16)
        total = dp_sum(ndp, ybuf, ysend, yrecv)
    out[...] = total.astype(out.dtype)

    def drain(j, carry):
        for k in range(nx):
            to_core(j, k).wait_send()
        for k in range(1, nx):
            to_x(j, k).wait_send()
        return carry

    lax.fori_loop(0, nz, drain, 0)
    for j in range(1, nz):
        to_z(j).wait_send()


def scatter_sum(part, nz, nx, ndp, dtype, collective_id):
    rows, cols = part.shape[0] // (nz * nx * 2), part.shape[1]
    block = (rows, cols)
    dma = pltpu.SemaphoreType.DMA
    spread = max(1, ndp - 1)
    return pl.pallas_call(
        functools.partial(scatter_kernel, nz, nx, ndp),
        out_shape=jax.ShapeDtypeStruct(block, dtype),
        in_specs=[pl.BlockSpec(memory_space=pltpu.VMEM)],
        out_specs=pl.BlockSpec(memory_space=pltpu.VMEM),
        scratch_shapes=[
            pltpu.VMEM((nz, nx) + block, jnp.bfloat16),
            pltpu.VMEM((nx - 1, nz) + block, jnp.bfloat16),
            pltpu.VMEM((nz - 1,) + block, jnp.bfloat16),
            pltpu.VMEM((ndp,) + block, jnp.bfloat16),
            dma((nz, nx)), dma((nz, nx)),
            dma((nx - 1, nz)), dma((nx - 1, nz)),
            dma((nz - 1,)), dma((nz - 1,)),
            dma((spread,)), dma((spread,)),
        ],
        compiler_params=pltpu.CompilerParams(
            collective_id=collective_id, has_side_effects=True, vmem_limit_bytes=VMEM_LIMIT
        ),
    )(part.reshape((nz, nx, 2) + block))


def gather_kernel(
    nz, nx, ndp, attn, tokens, gain, extra, out, residual, own, ybuf,
    ysend, yrecv, zsend, zrecv, xsend, xrecv, csend, crecv, local_sem,
):
    z, x, c = grid_place(nx)
    index = greet(nz, nx, ndp, z, x, c)
    width = tokens.shape[1]
    ybuf[lax.axis_index("dp")] = attn[...]
    resid = tokens[...].astype(jnp.float32) + dp_sum(ndp, ybuf, ysend, yrecv)
    residual[...] = resid
    own[:, :width] = norm_rows(resid, gain[...])
    own[:, width:] = extra[...]

    def block(j, k):
        return out.at[(z + nz - j) % nz, (x + nx - k) % nx, c]

    def to_z(j):
        return remote(own, out.at[z, x, c], zsend.at[j - 1], zrecv.at[j - 1], index((z + j) % nz, x, c))

    def to_x(src, j, k):
        return remote(
            src, block(j, 0), xsend.at[j, k - 1], xrecv.at[j, k - 1], index(z, (x + k) % nx, c)
        )

    def to_core(src, j, k):
        return remote(src, block(j, k), csend.at[j, k], crecv.at[j, k], index(z, x, 1 - c))

    keep = pltpu.make_async_copy(own, out.at[z, x, c], local_sem)
    keep.start()
    for j in range(1, nz):
        to_z(j).start()
    for k in range(1, nx):
        to_x(own, 0, k).start()
    to_core(own, 0, 0).start()

    def z_step(j, carry):
        to_z(j).wait_recv()
        for k in range(1, nx):
            to_x(block(j, 0), j, k).start()
        to_core(block(j, 0), j, 0).start()
        return carry

    def x_step(j, carry):
        for k in range(1, nx):
            to_x(own, j, k).wait_recv()
            to_core(block(j, k), j, k).start()
        return carry

    def core_step(j, carry):
        for k in range(nx):
            to_core(own, j, k).wait_recv()
        for k in range(nx):
            to_core(own, j, k).wait_send()
        for k in range(1, nx):
            to_x(own, j, k).wait_send()
        return carry

    lax.fori_loop(1, nz, z_step, 0)
    lax.fori_loop(0, nz, x_step, 0)
    lax.fori_loop(0, nz, core_step, 0)
    for j in range(1, nz):
        to_z(j).wait_send()
    keep.wait()


def gather_normed(attn, tokens, gain, extra, nz, nx, ndp, collective_id):
    rows, width = tokens.shape
    cols = width + extra.shape[1]
    dma = pltpu.SemaphoreType.DMA
    whole = pl.BlockSpec(memory_space=pltpu.VMEM)
    out, residual = pl.pallas_call(
        functools.partial(gather_kernel, nz, nx, ndp),
        out_shape=(
            jax.ShapeDtypeStruct((nz, nx, 2, rows, cols), jnp.bfloat16),
            jax.ShapeDtypeStruct((rows, width), jnp.float32),
        ),
        in_specs=[whole] * 4,
        out_specs=(pl.BlockSpec(memory_space=pl.ANY), whole),
        scratch_shapes=[
            pltpu.VMEM((rows, cols), jnp.bfloat16),
            pltpu.VMEM((ndp, rows, width), jnp.bfloat16),
            dma((ndp - 1,)), dma((ndp - 1,)),
            dma((nz - 1,)), dma((nz - 1,)),
            dma((nz, nx - 1)), dma((nz, nx - 1)),
            dma((nz, nx)), dma((nz, nx)),
            dma,
        ],
        compiler_params=pltpu.CompilerParams(
            collective_id=collective_id, has_side_effects=True, vmem_limit_bytes=VMEM_LIMIT
        ),
    )(attn, tokens, gain.reshape(1, width), extra)
    return out.reshape(nz * nx * 2 * rows, cols), residual


def attention_kernel(query, new_key, new_value, key, value, mask, fresh_mask, out):
    def scored(keys, valid):
        scores = lax.dot_general(
            query[...], keys, (((1,), (1,)), ((), ())), preferred_element_type=jnp.float32
        ) * HD ** (-0.5)
        return jnp.where(valid > 0, scores, -1e30)

    old = scored(key[...], mask[...])
    new = scored(new_key[...], fresh_mask[...])
    highest = jnp.maximum(
        jnp.max(old, axis=-1, keepdims=True), jnp.max(new, axis=-1, keepdims=True)
    )
    old, new = jnp.exp(old - highest), jnp.exp(new - highest)
    total = jnp.sum(old, axis=-1, keepdims=True) + jnp.sum(new, axis=-1, keepdims=True)
    old, new = (old / total).astype(jnp.bfloat16), (new / total).astype(jnp.bfloat16)
    out[...] = (
        jnp.dot(old, value[...], preferred_element_type=jnp.float32)
        + jnp.dot(new, new_value[...], preferred_element_type=jnp.float32)
    ).astype(jnp.bfloat16)


def attention(qkv, cache, valid, heads):
    rows, kept = qkv.shape[0], cache.shape[0]

    def columns(count, first):
        return pl.BlockSpec((count, HD), lambda h: (0, first + h))

    def fixed(width):
        return pl.BlockSpec((rows, width), lambda h: (0, 0))

    return pl.pallas_call(
        attention_kernel,
        grid=(heads,),
        out_shape=jax.ShapeDtypeStruct((rows, heads * HD), jnp.bfloat16),
        in_specs=[
            columns(rows, 0), columns(rows, heads), columns(rows, 2 * heads),
            columns(kept, 0), columns(kept, heads), fixed(kept), fixed(rows),
        ],
        out_specs=columns(rows, 0),
        compiler_params=pltpu.CompilerParams(vmem_limit_bytes=VMEM_LIMIT),
    )(qkv, qkv, qkv, cache, cache, valid[:, :kept], valid[:, kept:])


def in_pieces(values):
    pieces = []
    for _ in range(3):
        top = lax.reduce_precision(values, 8, 7)
        pieces.append(top.astype(jnp.bfloat16))
        values = values - top
    return pieces


def local(
    tokens,
    attn_gain,
    w_query,
    w_key,
    w_value,
    w_out,
    cache,
    page_table,
    cache_len,
    new_len,
    kv_owner,
    moe_gain,
    w_gate,
    w_up,
    w_down,
    expert_ids,
    gate_weights,
):
    row_count, model_width = tokens.shape
    n_expert, ndp = lax.axis_size("expert"), lax.axis_size("dp")
    nx, nz = ndp, n_expert // (2 * ndp)
    local_experts = w_gate.shape[0]
    experts_all = n_expert * local_experts
    kv_cap = max(2, 2 * row_count // n_expert)
    heads = w_query.shape[1] // HD
    depth = w_query.shape[0]
    full_out = lax.all_gather(w_out, "expert", axis=0, tiled=True)
    normed = norm_rows(tokens.astype(jnp.float32), attn_gain)
    strips = normed.reshape(row_count, n_expert, depth).transpose(1, 0, 2)
    strips = lax.all_to_all(strips, "expert", split_axis=0, concat_axis=0, tiled=True)
    strips = strips.reshape(n_expert * row_count, depth)
    terms = jnp.dot(
        strips,
        jnp.concatenate([w_query, w_key, w_value], axis=1),
        preferred_element_type=jnp.float32,
    ).astype(jnp.bfloat16)
    qkv = scatter_sum(terms, nz, nx, 1, jnp.bfloat16, 1)
    valid = key_masks(page_table[0], cache_len[0], new_len[0], row_count, PAGE)
    heads_out = attention(qkv, cache, valid.astype(jnp.int32), heads)
    attn_part = jnp.einsum(
        "tc,dc->td", heads_out, full_out, preferred_element_type=jnp.float32
    ).astype(jnp.bfloat16)
    labels = jnp.arange(experts_all, dtype=jnp.int32)
    gates = jnp.sum(
        jnp.where(expert_ids[:, :, None] == labels, gate_weights[:, :, None], 0.0), axis=1
    )
    extra = jnp.concatenate(in_pieces(gates), axis=1)
    extra = jnp.pad(extra, ((0, 0), (0, -extra.shape[1] % 128)))
    packed, residual = gather_normed(attn_part, tokens, moe_gain, extra, nz, nx, ndp, 2)
    kv_row = qkv[:, heads * HD :]
    kv_slot = kv_owner[:, 0] * kv_cap + owner_rank(kv_owner[:, 0])
    slots = jnp.arange(n_expert * kv_cap, dtype=jnp.int32)
    kv_buffer = jnp.dot(
        (slots[:, None] == kv_slot[None, :]).astype(jnp.bfloat16),
        kv_row,
        preferred_element_type=jnp.float32,
    ).astype(jnp.bfloat16)
    new_rows = lax.all_to_all(
        kv_buffer.reshape(n_expert, kv_cap, -1), "expert", split_axis=0, concat_axis=0, tiled=True
    ).reshape(n_expert * kv_cap, -1)
    rows = packed[:, :model_width]
    all_gates = packed[:, model_width : model_width + 3 * experts_all].astype(jnp.float32)
    all_gates = all_gates.reshape(-1, 3, experts_all)
    all_gates = all_gates[:, 0] + (all_gates[:, 1] + all_gates[:, 2])
    first = lax.axis_index("expert") * local_experts
    gated = 0.0
    for local_id in range(local_experts):
        gate_proj = jnp.dot(rows, w_gate[local_id], preferred_element_type=jnp.float32)
        up_proj = jnp.dot(rows, w_up[local_id], preferred_element_type=jnp.float32)
        active = (jax.nn.silu(gate_proj) * up_proj).astype(jnp.bfloat16)
        part = jnp.dot(active, w_down[local_id], preferred_element_type=jnp.float32)
        part = part.astype(jnp.bfloat16).astype(jnp.float32)
        mine = jnp.sum(jnp.where(labels == first + local_id, all_gates, 0.0), axis=1)
        gated = gated + part * mine[:, None]
    moe_total = scatter_sum(gated.astype(jnp.bfloat16), nz, nx, ndp, jnp.float32, 3)
    out = (residual + moe_total).astype(jnp.bfloat16)
    return (out, new_rows)


def solution(mesh):
    placed = (
        P("expert", None),
        P(),
        P("expert", "dp"),
        P("expert", "dp"),
        P("expert", "dp"),
        P("expert", "dp"),
        P("expert", "dp"),
        P("expert", None),
        P("expert", None),
        P("expert", None),
        P("expert", None),
        P(),
        P("expert", None, "dp"),
        P("expert", None, "dp"),
        P("expert", "dp", None),
        P("expert", None),
        P("expert", None),
    )
    return jax.shard_map(
        local,
        mesh=mesh,
        in_specs=placed,
        out_specs=(P("expert", None), P("expert", "dp")),
        check_vma=False,
    )
```

```python
import functools

import jax
import jax.numpy as jnp
from jax import lax
from jax.experimental import pallas as pl
from jax.experimental.pallas import tpu as pltpu
from jax.sharding import PartitionSpec as P

HD = 128
PAGE = 128
VMEM_LIMIT = 56 * 1024 * 1024


EPSILON = 1e-05


def norm_rows(row_data, gain_vec):
    mean_sq = jnp.mean(row_data * row_data, axis=-1, keepdims=True)
    return (row_data * lax.rsqrt(mean_sq + EPSILON) * gain_vec).astype(jnp.bfloat16)


def owner_rank(owners):
    ids = jnp.arange(owners.shape[0], dtype=jnp.int32)
    same = (owners[:, None] == owners[None, :]) & (ids[None, :] < ids[:, None])
    return jnp.sum(same.astype(jnp.int32), axis=1)


def key_masks(table_row, cache_lens, new_lens, row_count, page_size):
    req_count = cache_lens.shape[0]
    pages_here = table_row.shape[0]
    per_request = pages_here // req_count
    slot_ids = jnp.arange(pages_here, dtype=jnp.int32)
    matches = (table_row[:, None] == slot_ids[None, :]).astype(jnp.int32)
    slot_of_page = jnp.sum(matches * slot_ids[:, None], axis=0)
    page_request = slot_of_page // per_request
    page_start = slot_of_page % per_request * page_size
    key_request = jnp.repeat(page_request, page_size)
    key_position = jnp.repeat(page_start, page_size) + jnp.tile(
        jnp.arange(page_size, dtype=jnp.int32), pages_here
    )
    request_ids = jnp.arange(req_count, dtype=jnp.int32)
    key_length = jnp.sum(
        (key_request[:, None] == request_ids[None, :]).astype(jnp.int32) * cache_lens[None, :],
        axis=1,
    )
    request_ends = jnp.sum(
        jnp.where(request_ids[None, :] <= request_ids[:, None], new_lens[None, :], 0), axis=1
    )
    tok_ids = jnp.arange(row_count, dtype=jnp.int32)
    tok_request = jnp.sum((tok_ids[:, None] >= request_ends[None, :]).astype(jnp.int32), axis=1)
    cached = (tok_request[:, None] == key_request[None, :]) & (key_position < key_length)[None, :]
    fresh_mask = tok_request[:, None] == tok_request[None, :]
    return jnp.concatenate([cached, fresh_mask], axis=1)


def grid_place(nx):
    me = lax.axis_index("expert")
    return me // (2 * nx), (me // 2) % nx, me % 2


def remote(src, dst, send_sem, recv_sem, device):
    return pltpu.make_async_remote_copy(
        src_ref=src,
        dst_ref=dst,
        send_sem=send_sem,
        recv_sem=recv_sem,
        device_id=device,
        device_id_type=pl.DeviceIdType.MESH,
    )


def greet(nz, nx, ndp, z, x, c):
    def index(z_to, x_to, c_to):
        return (lax.axis_index("dp"), (z_to * nx + x_to) * 2 + c_to)

    barrier = pltpu.get_barrier_semaphore()
    peers = [index(z, x, 1 - c)]
    peers += [index(z, (x + k) % nx, c) for k in range(1, nx)]
    peers += [index((z + k) % nz, x, c) for k in range(1, nz)]
    peers += [
        ((lax.axis_index("dp") + k) % ndp, lax.axis_index("expert")) for k in range(1, ndp)
    ]
    for peer in peers:
        pl.semaphore_signal(barrier, inc=1, device_id=peer, device_id_type=pl.DeviceIdType.MESH)
    pl.semaphore_wait(barrier, len(peers))
    return index


def dp_sum(ndp, ybuf, ysend, yrecv):
    mine = lax.axis_index("dp")
    expert = lax.axis_index("expert")
    copies = []
    for k in range(1, ndp):
        copy = remote(
            ybuf.at[mine],
            ybuf.at[mine],
            ysend.at[k - 1],
            yrecv.at[k - 1],
            ((mine + k) % ndp, expert),
        )
        copy.start()
        copies.append(copy)
    for copy in copies:
        copy.wait()
    total = ybuf[0].astype(jnp.float32)
    for d in range(1, ndp):
        total = total + ybuf[d].astype(jnp.float32)
    return total


def scatter_kernel(
    nz, nx, ndp, part, out, cbuf, xbuf, zbuf, ybuf,
    csend, crecv, xsend, xrecv, zsend, zrecv, ysend, yrecv,
):
    z, x, c = grid_place(nx)
    index = greet(nz, nx, ndp, z, x, c)

    def to_core(j, k):
        zz, xx = (z + j) % nz, (x + k) % nx
        return remote(
            part.at[zz, xx, 1 - c], cbuf.at[zz, xx], csend.at[j, k], crecv.at[j, k],
            index(z, x, 1 - c),
        )

    def to_x(j, k):
        zz, xx = (z + j) % nz, (x + k) % nx
        return remote(
            cbuf.at[zz, xx], xbuf.at[k - 1, zz], xsend.at[k - 1, j], xrecv.at[k - 1, j],
            index(z, xx, c),
        )

    def to_z(j):
        zz = (z + j) % nz
        return remote(
            cbuf.at[zz, x], zbuf.at[j - 1], zsend.at[j - 1], zrecv.at[j - 1], index(zz, x, c)
        )

    def order(i):
        return (i + 1) % nz

    def start_core(i, carry):
        for k in range(1, nx):
            to_core(order(i), k).start()
        return carry

    def start_own(i, carry):
        to_core(order(i), 0).start()
        return carry

    def x_step(i, carry):
        j = order(i)
        zz = (z + j) % nz
        for k in range(1, nx):
            xx = (x + k) % nx
            to_core(j, k).wait_recv()
            summed = cbuf[zz, xx].astype(jnp.float32) + part[zz, xx, c].astype(jnp.float32)
            cbuf[zz, xx] = summed.astype(jnp.bfloat16)
            to_x(j, k).start()
        return carry

    def column(j):
        zz = (z + j) % nz
        to_core(j, 0).wait_recv()
        summed = cbuf[zz, x].astype(jnp.float32) + part[zz, x, c].astype(jnp.float32)
        for k in range(1, nx):
            to_x(j, k).wait_recv()
            summed = summed + xbuf[k - 1, zz].astype(jnp.float32)
        return zz, summed

    def z_step(j, carry):
        zz, summed = column(j)
        cbuf[zz, x] = summed.astype(jnp.bfloat16)
        to_z(j).start()
        return carry

    lax.fori_loop(0, nz, start_core, 0)
    lax.fori_loop(0, nz, start_own, 0)
    lax.fori_loop(0, nz, x_step, 0)
    lax.fori_loop(1, nz, z_step, 0)
    _, total = column(0)
    for j in range(1, nz):
        to_z(j).wait_recv()
        total = total + zbuf[j - 1].astype(jnp.float32)
    if ndp > 1:
        ybuf[lax.axis_index("dp")] = total.astype(jnp.bfloat16)
        total = dp_sum(ndp, ybuf, ysend, yrecv)
    out[...] = total.astype(out.dtype)

    def drain(j, carry):
        for k in range(nx):
            to_core(j, k).wait_send()
        for k in range(1, nx):
            to_x(j, k).wait_send()
        return carry

    lax.fori_loop(0, nz, drain, 0)
    for j in range(1, nz):
        to_z(j).wait_send()


def scatter_sum(part, nz, nx, ndp, dtype, collective_id):
    rows, cols = part.shape[0] // (nz * nx * 2), part.shape[1]
    block = (rows, cols)
    dma = pltpu.SemaphoreType.DMA
    spread = max(1, ndp - 1)
    return pl.pallas_call(
        functools.partial(scatter_kernel, nz, nx, ndp),
        out_shape=jax.ShapeDtypeStruct(block, dtype),
        in_specs=[pl.BlockSpec(memory_space=pltpu.VMEM)],
        out_specs=pl.BlockSpec(memory_space=pltpu.VMEM),
        scratch_shapes=[
            pltpu.VMEM((nz, nx) + block, jnp.bfloat16),
            pltpu.VMEM((nx - 1, nz) + block, jnp.bfloat16),
            pltpu.VMEM((nz - 1,) + block, jnp.bfloat16),
            pltpu.VMEM((ndp,) + block, jnp.bfloat16),
            dma((nz, nx)), dma((nz, nx)),
            dma((nx - 1, nz)), dma((nx - 1, nz)),
            dma((nz - 1,)), dma((nz - 1,)),
            dma((spread,)), dma((spread,)),
        ],
        compiler_params=pltpu.CompilerParams(
            collective_id=collective_id, has_side_effects=True, vmem_limit_bytes=VMEM_LIMIT
        ),
    )(part.reshape((nz, nx, 2) + block))


def gather_kernel(
    nz, nx, ndp, attn, tokens, gain, extra, out, residual, own, ybuf,
    ysend, yrecv, zsend, zrecv, xsend, xrecv, csend, crecv, local_sem,
):
    z, x, c = grid_place(nx)
    index = greet(nz, nx, ndp, z, x, c)
    width = tokens.shape[1]
    ybuf[lax.axis_index("dp")] = attn[...]
    resid = tokens[...].astype(jnp.float32) + dp_sum(ndp, ybuf, ysend, yrecv)
    residual[...] = resid
    own[:, :width] = norm_rows(resid, gain[...])
    own[:, width:] = extra[...]

    def block(j, k):
        return out.at[(z + nz - j) % nz, (x + nx - k) % nx, c]

    def to_z(j):
        return remote(own, out.at[z, x, c], zsend.at[j - 1], zrecv.at[j - 1], index((z + j) % nz, x, c))

    def to_x(src, j, k):
        return remote(
            src, block(j, 0), xsend.at[j, k - 1], xrecv.at[j, k - 1], index(z, (x + k) % nx, c)
        )

    def to_core(src, j, k):
        return remote(src, block(j, k), csend.at[j, k], crecv.at[j, k], index(z, x, 1 - c))

    keep = pltpu.make_async_copy(own, out.at[z, x, c], local_sem)
    keep.start()
    for j in range(1, nz):
        to_z(j).start()
    for k in range(1, nx):
        to_x(own, 0, k).start()
    to_core(own, 0, 0).start()

    def z_step(j, carry):
        to_z(j).wait_recv()
        for k in range(1, nx):
            to_x(block(j, 0), j, k).start()
        to_core(block(j, 0), j, 0).start()
        return carry

    def x_step(j, carry):
        for k in range(1, nx):
            to_x(own, j, k).wait_recv()
            to_core(block(j, k), j, k).start()
        return carry

    def core_step(j, carry):
        for k in range(nx):
            to_core(own, j, k).wait_recv()
        for k in range(nx):
            to_core(own, j, k).wait_send()
        for k in range(1, nx):
            to_x(own, j, k).wait_send()
        return carry

    lax.fori_loop(1, nz, z_step, 0)
    lax.fori_loop(0, nz, x_step, 0)
    lax.fori_loop(0, nz, core_step, 0)
    for j in range(1, nz):
        to_z(j).wait_send()
    keep.wait()


def gather_normed(attn, tokens, gain, extra, nz, nx, ndp, collective_id):
    rows, width = tokens.shape
    cols = width + extra.shape[1]
    dma = pltpu.SemaphoreType.DMA
    whole = pl.BlockSpec(memory_space=pltpu.VMEM)
    out, residual = pl.pallas_call(
        functools.partial(gather_kernel, nz, nx, ndp),
        out_shape=(
            jax.ShapeDtypeStruct((nz, nx, 2, rows, cols), jnp.bfloat16),
            jax.ShapeDtypeStruct((rows, width), jnp.float32),
        ),
        in_specs=[whole] * 4,
        out_specs=(whole, whole),
        scratch_shapes=[
            pltpu.VMEM((rows, cols), jnp.bfloat16),
            pltpu.VMEM((ndp, rows, width), jnp.bfloat16),
            dma((ndp - 1,)), dma((ndp - 1,)),
            dma((nz - 1,)), dma((nz - 1,)),
            dma((nz, nx - 1)), dma((nz, nx - 1)),
            dma((nz, nx)), dma((nz, nx)),
            dma,
        ],
        compiler_params=pltpu.CompilerParams(
            collective_id=collective_id, has_side_effects=True, vmem_limit_bytes=VMEM_LIMIT
        ),
    )(attn, tokens, gain.reshape(1, width), extra)
    return out.reshape(nz * nx * 2 * rows, cols), residual


def attention_kernel(query, new_key, new_value, key, value, mask, fresh_mask, out):
    def scored(keys, valid):
        scores = lax.dot_general(
            query[...], keys, (((1,), (1,)), ((), ())), preferred_element_type=jnp.float32
        ) * HD ** (-0.5)
        return jnp.where(valid > 0, scores, -1e30)

    old = scored(key[...], mask[...])
    new = scored(new_key[...], fresh_mask[...])
    highest = jnp.maximum(
        jnp.max(old, axis=-1, keepdims=True), jnp.max(new, axis=-1, keepdims=True)
    )
    old, new = jnp.exp(old - highest), jnp.exp(new - highest)
    total = jnp.sum(old, axis=-1, keepdims=True) + jnp.sum(new, axis=-1, keepdims=True)
    old, new = (old / total).astype(jnp.bfloat16), (new / total).astype(jnp.bfloat16)
    out[...] = (
        jnp.dot(old, value[...], preferred_element_type=jnp.float32)
        + jnp.dot(new, new_value[...], preferred_element_type=jnp.float32)
    ).astype(jnp.bfloat16)


def attention(qkv, cache, valid, heads):
    rows, kept = qkv.shape[0], cache.shape[0]

    def columns(count, first):
        return pl.BlockSpec((count, HD), lambda h: (0, first + h))

    def fixed(width):
        return pl.BlockSpec((rows, width), lambda h: (0, 0))

    return pl.pallas_call(
        attention_kernel,
        grid=(heads,),
        out_shape=jax.ShapeDtypeStruct((rows, heads * HD), jnp.bfloat16),
        in_specs=[
            columns(rows, 0), columns(rows, heads), columns(rows, 2 * heads),
            columns(kept, 0), columns(kept, heads), fixed(kept), fixed(rows),
        ],
        out_specs=columns(rows, 0),
        compiler_params=pltpu.CompilerParams(vmem_limit_bytes=VMEM_LIMIT),
    )(qkv, qkv, qkv, cache, cache, valid[:, :kept], valid[:, kept:])


def in_pieces(values):
    pieces = []
    for _ in range(3):
        top = lax.reduce_precision(values, 8, 7)
        pieces.append(top.astype(jnp.bfloat16))
        values = values - top
    return pieces


def local(
    tokens,
    attn_gain,
    w_query,
    w_key,
    w_value,
    w_out,
    cache,
    page_table,
    cache_len,
    new_len,
    kv_owner,
    moe_gain,
    w_gate,
    w_up,
    w_down,
    expert_ids,
    gate_weights,
):
    row_count, model_width = tokens.shape
    n_expert, ndp = lax.axis_size("expert"), lax.axis_size("dp")
    nx, nz = ndp, n_expert // (2 * ndp)
    local_experts = w_gate.shape[0]
    experts_all = n_expert * local_experts
    kv_cap = max(2, 2 * row_count // n_expert)
    heads = w_query.shape[1] // HD
    depth = w_query.shape[0]
    full_out = lax.all_gather(w_out, "expert", axis=0, tiled=True)
    normed = norm_rows(tokens.astype(jnp.float32), attn_gain)
    strips = normed.reshape(row_count, n_expert, depth).transpose(1, 0, 2)
    strips = lax.all_to_all(strips, "expert", split_axis=0, concat_axis=0, tiled=True)
    strips = strips.reshape(n_expert * row_count, depth)
    terms = jnp.dot(
        strips,
        jnp.concatenate([w_query, w_key, w_value], axis=1),
        preferred_element_type=jnp.float32,
    ).astype(jnp.bfloat16)
    qkv = scatter_sum(terms, nz, nx, 1, jnp.bfloat16, 1)
    valid = key_masks(page_table[0], cache_len[0], new_len[0], row_count, PAGE)
    heads_out = attention(qkv, cache, valid.astype(jnp.int32), heads)
    attn_part = jnp.einsum(
        "tc,dc->td", heads_out, full_out, preferred_element_type=jnp.float32
    ).astype(jnp.bfloat16)
    labels = jnp.arange(experts_all, dtype=jnp.int32)
    gates = jnp.sum(
        jnp.where(expert_ids[:, :, None] == labels, gate_weights[:, :, None], 0.0), axis=1
    )
    extra = jnp.concatenate(in_pieces(gates), axis=1)
    extra = jnp.pad(extra, ((0, 0), (0, -extra.shape[1] % 128)))
    packed, residual = gather_normed(attn_part, tokens, moe_gain, extra, nz, nx, ndp, 2)
    kv_row = qkv[:, heads * HD :]
    kv_slot = kv_owner[:, 0] * kv_cap + owner_rank(kv_owner[:, 0])
    slots = jnp.arange(n_expert * kv_cap, dtype=jnp.int32)
    kv_buffer = jnp.dot(
        (slots[:, None] == kv_slot[None, :]).astype(jnp.bfloat16),
        kv_row,
        preferred_element_type=jnp.float32,
    ).astype(jnp.bfloat16)
    new_rows = lax.all_to_all(
        kv_buffer.reshape(n_expert, kv_cap, -1), "expert", split_axis=0, concat_axis=0, tiled=True
    ).reshape(n_expert * kv_cap, -1)
    rows = packed[:, :model_width]
    all_gates = packed[:, model_width : model_width + 3 * experts_all].astype(jnp.float32)
    all_gates = all_gates.reshape(-1, 3, experts_all)
    all_gates = all_gates[:, 0] + (all_gates[:, 1] + all_gates[:, 2])
    first = lax.axis_index("expert") * local_experts
    gated = 0.0
    for local_id in range(local_experts):
        gate_proj = jnp.dot(rows, w_gate[local_id], preferred_element_type=jnp.float32)
        up_proj = jnp.dot(rows, w_up[local_id], preferred_element_type=jnp.float32)
        active = (jax.nn.silu(gate_proj) * up_proj).astype(jnp.bfloat16)
        part = jnp.dot(active, w_down[local_id], preferred_element_type=jnp.float32)
        part = part.astype(jnp.bfloat16).astype(jnp.float32)
        mine = jnp.sum(jnp.where(labels == first + local_id, all_gates, 0.0), axis=1)
        gated = gated + part * mine[:, None]
    moe_total = scatter_sum(gated.astype(jnp.bfloat16), nz, nx, ndp, jnp.float32, 3)
    out = (residual + moe_total).astype(jnp.bfloat16)
    return (out, new_rows)


def solution(mesh):
    placed = (
        P("expert", None),
        P(),
        P("expert", "dp"),
        P("expert", "dp"),
        P("expert", "dp"),
        P("expert", "dp"),
        P("expert", "dp"),
        P("expert", None),
        P("expert", None),
        P("expert", None),
        P("expert", None),
        P(),
        P("expert", None, "dp"),
        P("expert", None, "dp"),
        P("expert", "dp", None),
        P("expert", None),
        P("expert", None),
    )
    return jax.shard_map(
        local,
        mesh=mesh,
        in_specs=placed,
        out_specs=(P("expert", None), P("expert", "dp")),
        check_vma=False,
    )
```
